32 devices in a mesh: groups: 2 (over y), dom: 4 (over z), edge: 2 (over x), sub: 2 (over core).
Axes of the slice: x: 2, y: 2, z: 4, core: 2. Of those that a mesh axis runs over, the one named last changes fastest.
Arguments:
- node_lat: bfloat16 [4096, 128], P(('groups', 'dom', 'edge', 'sub')), parts along dimension 0, may hold values from -6 to 6
- edge_lat: bfloat16 [32768, 128], P(('groups', 'dom', 'edge', 'sub')), parts along dimension 0, may hold values from -6 to 6
- node_cot: bfloat16 [4096, 128], P(('groups', 'dom', 'edge', 'sub')), parts along dimension 0, may hold values from -6 to 6
- edge_cot: bfloat16 [32768, 128], P(('groups', 'dom', 'edge', 'sub')), parts along dimension 0, may hold values from -6 to 6
- senders: int32 [32768], P(('groups', 'dom', 'edge', 'sub')), parts along dimension 0, may hold values from 0 to 1023, as said below
- receivers: int32 [32768], P(('groups', 'dom', 'edge', 'sub')), parts along dimension 0, may hold values from 0 to 511
- send_idx: int32 [8, 4, 128], P(('groups', 'dom')), parts along dimension 0, may hold values from 0 to 511, as said below
- send_len: int32 [8, 4], P(('groups', 'dom')), parts along dimension 0, may hold values from 0 to 128, as said below
- edge_count: int32 [8, 4], P(('groups', 'dom'), ('edge', 'sub')), parts along dimension 0, may hold values from 512 to 1024, as said below
- edge_weights: bfloat16 [5, 128, 128], replicated, may hold values from -0.375 to 0.375
- edge_bias: float32 [3, 128], replicated, may hold values from -3 to 3
- edge_gain: float32 [128], replicated, may hold values from 0.1 to 1.9
- edge_shift: float32 [128], replicated, may hold values from -3 to 3
- node_weights: bfloat16 [4, 128, 128], replicated, may hold values from -0.375 to 0.375
- node_bias: float32 [3, 128], replicated, may hold values from -3 to 3
- node_gain: float32 [128], replicated, may hold values from 0.1 to 1.9
Outputs:
- grad_nodes: float32 [4096, 128], P(('groups', 'dom', 'edge', 'sub')), parts along dimension 0
- grad_edges: bfloat16 [32768, 128], P(('groups', 'dom', 'edge', 'sub')), parts along dimension 0
- grad_edge_weights: float32 [10, 128, 128], P('groups'), parts along dimension 0
- grad_edge_vecs: float32 [10, 128], P('groups'), parts along dimension 0
- grad_node_weights: float32 [8, 128, 128], P('groups'), parts along dimension 0
- grad_node_vecs: float32 [8, 128], P('groups'), parts along dimension 0
The draws below stay inside these ranges and needn't reach their ends.
There are 2 independent parts, one for each index of `groups`. The reference program is written for one: setup_inputs(seed, part) draws one part's arguments, and reference() takes and returns one part's arrays. A program takes and returns all parts, laid end to end along the dimension named above; an argument that names none is the same for every part. Nothing has to cross between parts.
Inputs may be any that keep to these rules, and one draw needn't show every extreme that they name: `send_idx`: local node rows of the sending part; entries at or past send_len are not sent. `send_len`: zero where part p + o_k does not exist; some list holds 128 rows in every draw. `senders`: below 512: an own node row of the edge's part; else 512 + k * 128 + j with j below send_len[p - o_k, k]. `edge_count`: every part has a device with all 1024 rows in use.
All inputs are finite; a program needn't handle non-finite values.
Results may differ from the reference program's by a relative error of at most 0.0093.
Values may be sent and summed in bfloat16 or wider, within the bound.
A program may use at most 64 MiB of HBM per device.

```python
import math
import jax
import jax.numpy as jnp
from jax import lax

LAT = 128
EDGE_DEV = 1024
NEAR = 2
SLOT = 128
NODE_PART = 512
NODES = 2048
EDGE_PART = 4096
EDGES = 16384
N_DOM = 4
N_EDGE = 2
N_SUB = 2


def neighbour_offsets():
    return jnp.array([block_id - NEAR if block_id < NEAR else block_id - NEAR + 1 for block_id in range(2 * NEAR)], jnp.int32)


def halo_lengths(key):
    lengths_key = jax.random.fold_in(key, 41)
    lengths = jax.random.randint(lengths_key, (N_DOM, 2 * NEAR), SLOT // 4, SLOT + 1)
    target = jnp.arange(N_DOM, dtype=jnp.int32)[:, None] + neighbour_offsets()[None, :]
    lengths = jnp.where((target >= 0) & (target < N_DOM), lengths, 0)
    return lengths.at[0, 2 * NEAR - 1].set(SLOT).astype(jnp.int32)


def draw_send_len(key, part):
    return halo_lengths(key)


def draw_send_idx(key, part):
    key = jax.random.fold_in(key, 5)
    return jax.random.randint(key, (N_DOM, 2 * NEAR, SLOT), 0, NODE_PART).astype(jnp.int32)


def draw_senders(key, part):
    lengths = halo_lengths(key)
    key = jax.random.fold_in(key, 3)
    source = jnp.arange(N_DOM, dtype=jnp.int32)[:, None] - neighbour_offsets()[None, :]
    inside = (source >= 0) & (source < N_DOM)
    clipped = jnp.clip(source, 0, N_DOM - 1)
    recv_len = jnp.where(inside, lengths[clipped, jnp.arange(2 * NEAR, dtype=jnp.int32)[None, :]], 0)
    own_key, block_key, position_key, pick_key = jax.random.split(key, 4)
    own_rows = jax.random.randint(own_key, (N_DOM, EDGE_PART), 0, NODE_PART)
    block_ids = jax.random.randint(block_key, (N_DOM, EDGE_PART), 0, 2 * NEAR)
    position_draw = jax.random.randint(position_key, (N_DOM, EDGE_PART), 0, 1 << 20)
    halo_pick = jax.random.randint(pick_key, (N_DOM, EDGE_PART), 0, 5)
    block_len = jnp.take_along_axis(recv_len, block_ids, axis=1)
    halo_index = NODE_PART + block_ids * SLOT + position_draw % jnp.maximum(block_len, 1)
    result = jnp.where((halo_pick == 0) & (block_len > 0), halo_index, own_rows)
    result = result.at[NEAR, 0].set(NODE_PART + 2 * NEAR * SLOT - 1)
    return result.reshape(-1).astype(jnp.int32)


def draw_edge_count(key, part):
    key = jax.random.fold_in(key, 9)
    count_key, full_key = jax.random.split(key)
    devices_part = N_EDGE * N_SUB
    counts = jax.random.randint(count_key, (N_DOM, devices_part), EDGE_DEV // 2, EDGE_DEV + 1)
    full_device = jax.random.randint(full_key, (N_DOM,), 0, devices_part)
    column = jnp.arange(devices_part, dtype=jnp.int32)[None, :]
    return jnp.where(column == full_device[:, None], EDGE_DEV, counts).astype(jnp.int32)


def plant(values, key, low, high):
    dims = values.shape
    spot = [jax.random.randint(jax.random.fold_in(key, axis), (), 0, dims[axis]) for axis in range(len(dims))]
    values = values.at[tuple(spot)].set(low)
    longest = dims.index(max(dims))
    spot[longest] = (spot[longest] + 1) % dims[longest]
    return values.at[tuple(spot)].set(high)


def shard_levels(key, dims, pieces, low, largest):
    def one(position, blocks):
        heights = jax.random.uniform(jax.random.fold_in(jax.random.fold_in(key, 6), position), (blocks,), jnp.float32, low / len(pieces), largest / len(pieces))
        return jnp.repeat(jnp.exp(heights), dims[position] // blocks).reshape((-1,) + (1,) * (len(dims) - position - 1))

    level = one(*pieces[0])
    for cut in pieces[1:]:
        level = level * one(*cut)
    return level


def gaussian(stream_key, shape, width, limit, cuts=(), held_as=jnp.bfloat16):
    values = jax.random.normal(stream_key, shape, jnp.float32) * width
    if len(cuts) > 0:
        values = shard_levels(stream_key, shape, cuts, -0.22, 0.18) * values
    return jnp.clip(values, min=-limit, max=limit).astype(held_as)


def setup_inputs(seed: int = 0, part: int = 0) -> dict:
    key_of = jax.random.split(jax.random.key(seed), 17)
    own_keys = jax.random.split(jax.random.fold_in(key_of[16], part), 17)
    node_lat = gaussian(own_keys[0], (NODES, LAT), 1.0, 6.0, ((0, 16),))
    edge_lat = gaussian(own_keys[1], (EDGES, LAT), 1.0, 6.0, ((0, 16),))
    node_cot = gaussian(own_keys[2], (NODES, LAT), 1.0, 6.0, ((0, 16),))
    edge_cot = gaussian(own_keys[3], (EDGES, LAT), 1.0, 6.0, ((0, 16),))
    senders = draw_senders(jax.random.fold_in(jax.random.fold_in(key_of[16], part), 71), part)
    receivers = plant(jax.random.randint(own_keys[5], (EDGES,), 0, NODE_PART), jax.random.fold_in(own_keys[5], 1), 0, NODE_PART - 1).astype(jnp.int32)
    send_idx = draw_send_idx(jax.random.fold_in(jax.random.fold_in(key_of[16], part), 71), part)
    send_len = draw_send_len(jax.random.fold_in(jax.random.fold_in(key_of[16], part), 71), part)
    edge_count = draw_edge_count(jax.random.fold_in(jax.random.fold_in(key_of[16], part), 71), part)
    edge_weights = gaussian(key_of[9], (5, LAT, LAT), (2 * LAT) ** -0.5, 0.375)
    edge_bias = gaussian(key_of[10], (3, LAT), 0.5, 3.0, (), jnp.float32)
    edge_gain = jnp.clip(1.0 + 0.18 * jax.random.normal(key_of[11], (LAT,), jnp.float32), 0.1, 1.9)
    edge_shift = gaussian(key_of[12], (LAT,), 0.5, 3.0, (), jnp.float32)
    node_weights = gaussian(key_of[13], (4, LAT, LAT), (2 * LAT) ** -0.5, 0.375)
    node_bias = gaussian(key_of[14], (3, LAT), 0.5, 3.0, (), jnp.float32)
    node_gain = jnp.clip(1.0 + 0.18 * jax.random.normal(key_of[15], (LAT,), jnp.float32), 0.1, 1.9)
    return {"node_lat": node_lat, "edge_lat": edge_lat, "node_cot": node_cot, "edge_cot": edge_cot, "senders": senders, "receivers": receivers, "send_idx": send_idx, "send_len": send_len, "edge_count": edge_count, "edge_weights": edge_weights, "edge_bias": edge_bias, "edge_gain": edge_gain, "edge_shift": edge_shift, "node_weights": node_weights, "node_bias": node_bias, "node_gain": node_gain}


EPSILON = 1e-05

def silu_slope(values):
    sigmoid_value = jax.nn.sigmoid(values)
    return sigmoid_value * (1.0 + values * (1.0 - sigmoid_value))

def transposed(left_side, right_side):
    return lax.dot_general(left_side, right_side, (((0,), (0,)), ((), ())), preferred_element_type=jnp.float32)

def stack_forward(inputs, w_first, w_second, w_third, biases):
    first_pre = jnp.dot(inputs, w_first, preferred_element_type=jnp.float32) + biases[0]
    first_act = jax.nn.silu(first_pre).astype(jnp.bfloat16)
    second_pre = jnp.dot(first_act, w_second, preferred_element_type=jnp.float32) + biases[1]
    second_act = jax.nn.silu(second_pre).astype(jnp.bfloat16)
    third_pre = jnp.dot(second_act, w_third, preferred_element_type=jnp.float32) + biases[2]
    centred = third_pre - lax.optimization_barrier(jnp.mean(third_pre, axis=1, keepdims=True))
    inv_std = lax.rsqrt(lax.optimization_barrier(jnp.mean(centred * centred, axis=1, keepdims=True)) + EPSILON)
    return (first_pre, first_act, second_pre, second_act, centred * inv_std, inv_std)

def stack_backward(inputs, w_first, w_second, w_third, gains, stored, out_grad):
    first_pre, first_act, second_pre, second_act, normed, inv_std = stored
    scaled = out_grad * gains
    third_grad = inv_std * (scaled - lax.optimization_barrier(jnp.mean(scaled, axis=1, keepdims=True)) - normed * lax.optimization_barrier(jnp.mean(scaled * normed, axis=1, keepdims=True)))
    third_low = third_grad.astype(jnp.bfloat16)
    second_grad = jnp.dot(third_low, w_third.T, preferred_element_type=jnp.float32) * silu_slope(second_pre)
    second_low = second_grad.astype(jnp.bfloat16)
    first_grad = jnp.dot(second_low, w_second.T, preferred_element_type=jnp.float32) * silu_slope(first_pre)
    first_low = first_grad.astype(jnp.bfloat16)
    input_grad = jnp.dot(first_low, w_first.T, preferred_element_type=jnp.float32)
    weight_grads = (transposed(inputs, first_low), transposed(first_act, second_low), transposed(second_act, third_low))
    vector_grads = jnp.stack([lax.optimization_barrier(jnp.sum(first_grad, 0)), lax.optimization_barrier(jnp.sum(second_grad, 0)), lax.optimization_barrier(jnp.sum(third_grad, 0)), lax.optimization_barrier(jnp.sum(out_grad * normed, 0)), lax.optimization_barrier(jnp.sum(out_grad, 0))])
    return (input_grad, weight_grads, vector_grads)

def reference(node_lat, edge_lat, node_cot, edge_cot, senders, receivers, send_idx, send_len, edge_count, edge_weights, edge_bias, edge_gain, edge_shift, node_weights, node_bias, node_gain):
    features = LAT
    blocks = 2 * NEAR
    offsets = jnp.array([block_id - NEAR if block_id < NEAR else block_id - NEAR + 1 for block_id in range(blocks)], jnp.int32)
    part_nodes = node_lat.reshape(N_DOM, NODE_PART, features)
    source = jnp.arange(N_DOM, dtype=jnp.int32)[:, None] - offsets[None, :]
    inside = (source >= 0) & (source < N_DOM)
    clipped = jnp.clip(source, 0, N_DOM - 1).astype(jnp.int32)
    block_ids = jnp.arange(blocks, dtype=jnp.int32)[None, :]
    send_lists = send_idx[clipped, block_ids]
    lengths = jnp.where(inside, send_len[clipped, block_ids], 0)
    live_rows = jnp.arange(SLOT, dtype=jnp.int32)[None, None, :] < lengths[:, :, None]
    halo_rows = jnp.where(live_rows[..., None], part_nodes[clipped[:, :, None], send_lists], jnp.zeros((), jnp.bfloat16))
    extended = jnp.concatenate([part_nodes, halo_rows.reshape(N_DOM, blocks * SLOT, features)], axis=1)
    edge_valid = (jnp.arange(EDGE_DEV, dtype=jnp.int32)[None, None, :] < edge_count[:, :, None]).reshape(N_DOM, EDGE_PART)
    lat_parts = edge_lat.reshape(N_DOM, EDGE_PART, features)
    cot_parts = edge_cot.reshape(N_DOM, EDGE_PART, features)
    send_parts = senders.reshape(N_DOM, EDGE_PART)
    recv_parts = receivers.reshape(N_DOM, EDGE_PART)
    edge_first = edge_weights[:3].reshape(3 * features, features)

    def edge_inputs(ext_rows, lat_rows, send_rows, recv_rows):
        return jnp.concatenate([lat_rows, ext_rows[send_rows], ext_rows[recv_rows]], axis=1)

    def first_pass(packed):
        ext_rows, lat_rows, send_rows, recv_rows, valid_rows = packed
        stored = stack_forward(edge_inputs(ext_rows, lat_rows, send_rows, recv_rows), edge_first, edge_weights[3], edge_weights[4], edge_bias)
        edge_out = jnp.where(valid_rows[:, None], stored[4] * edge_gain + edge_shift, 0.0)
        return jax.ops.segment_sum(edge_out, recv_rows, num_segments=NODE_PART)
    summed_edges = lax.map(first_pass, (extended, lat_parts, send_parts, recv_parts, edge_valid))
    node_inputs = jnp.concatenate([node_lat, summed_edges.reshape(NODES, features).astype(jnp.bfloat16)], axis=1)
    node_first = node_weights[:2].reshape(2 * features, features)
    node_stored = stack_forward(node_inputs, node_first, node_weights[2], node_weights[3], node_bias)
    node_grad, node_wgrads, node_vgrads = stack_backward(node_inputs, node_first, node_weights[2], node_weights[3], node_gain, node_stored, node_cot.astype(jnp.float32))
    agg_grad = node_grad[:, features:].reshape(N_DOM, NODE_PART, features)

    def second_pass(packed):
        ext_rows, lat_rows, send_rows, recv_rows, valid_rows, agg_rows, cot_rows = packed
        inputs = edge_inputs(ext_rows, lat_rows, send_rows, recv_rows)
        stored = stack_forward(inputs, edge_first, edge_weights[3], edge_weights[4], edge_bias)
        cot_float = cot_rows.astype(jnp.float32)
        edge_dy = jnp.where(valid_rows[:, None], cot_float + agg_rows[recv_rows], 0.0)
        edge_grad, wgrads, vgrads = stack_backward(inputs, edge_first, edge_weights[3], edge_weights[4], edge_gain, stored, edge_dy)
        grad_rows = (cot_float + edge_grad[:, :features]).astype(jnp.bfloat16)
        ext_grad = jax.ops.segment_sum(edge_grad[:, features:2 * features], send_rows, num_segments=NODE_PART + blocks * SLOT)
        ext_grad = ext_grad.at[:NODE_PART].add(jax.ops.segment_sum(edge_grad[:, 2 * features:], recv_rows, num_segments=NODE_PART))
        return (grad_rows, ext_grad, wgrads, vgrads)
    grad_parts, ext_grads, edge_wparts, edge_vparts = lax.map(second_pass, (extended, lat_parts, send_parts, recv_parts, edge_valid, agg_grad, cot_parts))
    owned = ext_grads[:, :NODE_PART]
    halo_back = ext_grads[:, NODE_PART:].reshape(N_DOM, blocks, SLOT, features)
    owned = owned.at[clipped[:, :, None], send_lists].add(jnp.where(live_rows[..., None], halo_back, 0.0))
    grad_nodes = node_cot.astype(jnp.float32) + node_grad[:, :features] + owned.reshape(NODES, features)
    grad_edges = grad_parts.reshape(EDGES, features)
    edge_scale = 1.0 / math.sqrt(EDGES)
    node_scale = 1.0 / math.sqrt(NODES)
    edge_wsum = [lax.optimization_barrier(jnp.sum(part_grads, axis=0)) for part_grads in edge_wparts]
    grad_edge_weights = jnp.concatenate([edge_wsum[0].reshape(3, features, features), edge_wsum[1][None], edge_wsum[2][None]], axis=0) * edge_scale
    grad_edge_vecs = lax.optimization_barrier(jnp.sum(edge_vparts, axis=0)) * edge_scale
    grad_node_weights = jnp.concatenate([node_wgrads[0].reshape(2, features, features), node_wgrads[1][None], node_wgrads[2][None]], axis=0) * node_scale
    grad_node_vecs = node_vgrads[:4] * node_scale
    return (grad_nodes, grad_edges, grad_edge_weights, grad_edge_vecs, grad_node_weights, grad_node_vecs)
```

```python
import functools
import math

import jax
import jax.numpy as jnp
from jax import lax
from jax.experimental import pallas as pl
from jax.experimental.pallas import tpu as pltpu
from jax.sharding import PartitionSpec as P

EPSILON = 1e-05
F32 = jnp.float32
BF16 = jnp.bfloat16
LANES = 128
CHUNK = 256


def nn(left, right):
    return lax.dot_general(left, right, (((1,), (0,)), ((), ())), preferred_element_type=F32)


def nt(left, right):
    return lax.dot_general(left, right, (((1,), (1,)), ((), ())), preferred_element_type=F32)


def tn(left, right):
    return lax.dot_general(left, right, (((0,), (0,)), ((), ())), preferred_element_type=F32)


def sigmoid(values):
    return 0.5 * jnp.tanh(0.5 * values) + 0.5


def slope_of(values):
    gate = sigmoid(values)
    return gate * (1.0 + values * (1.0 - gate))


def silu(values):
    return values * sigmoid(values)


def normalise(pre):
    centred = pre - jnp.mean(pre, axis=1, keepdims=True)
    inv_std = lax.rsqrt(jnp.mean(centred * centred, axis=1, keepdims=True) + EPSILON)
    return centred * inv_std, inv_std


def norm_backward(scaled, normed, inv_std):
    return inv_std * (
        scaled
        - jnp.mean(scaled, axis=1, keepdims=True)
        - normed * jnp.mean(scaled * normed, axis=1, keepdims=True)
    )


def column_sum(values):
    return jnp.sum(values, axis=0, keepdims=True)


def kernel(
    sizes,
    node_lat,
    edge_lat,
    node_cot,
    edge_cot,
    senders,
    receivers,
    send_idx,
    send_len,
    edge_count,
    edge_w,
    edge_b,
    edge_g,
    edge_s,
    node_w,
    node_b,
    node_g,
    out_nodes,
    out_edges,
    out_ew,
    out_ev,
    out_nw,
    out_nv,
    ext,
    outgoing,
    oh_s,
    oht_s,
    oh_r,
    oht_r,
    oh_i,
    proj,
    z1,
    z2,
    a1,
    a2,
    normed_e,
    inv_e,
    low_y,
    sum_send,
    sum_recv,
    agg,
    agg_own,
    d1,
    d2,
    d3,
    back_send,
    back_recv,
    own_acc,
    own_send,
    own_recv,
    nw_stage,
    nw_recv,
    nw_zown,
    nw_z,
    nw_fown,
    nw_full,
    ew_stage,
    ew_recv,
    ew_zown,
    ew_z,
    ew_fown,
    ew_full,
    vec,
    vec_in,
    vec_zown,
    vec_z,
    ag_s,
    ag_r,
    halo_s,
    halo_r,
    sum_s,
    sum_r,
    agg_s,
    agg_r,
    back_s,
    back_r,
    own_s,
    own_r,
    nrs_s,
    nrs_r,
    nz_s,
    nz_r,
    nag_s,
    nag_r,
    ers_s,
    ers_r,
    ez_s,
    ez_r,
    eag_s,
    eag_r,
    vrs_s,
    vrs_r,
    vz_s,
    vz_r,
):
    dom, n_edge, n_sub = sizes
    inner = n_edge * n_sub
    rows = node_lat.shape[0]
    edges = edge_lat.shape[0]
    part_rows = rows * inner
    blocks, slot = send_idx.shape
    ext_rows = part_rows + blocks * slot
    reach = blocks // 2
    offsets = [b - reach if b < reach else b - reach + 1 for b in range(blocks)]
    my_dom = lax.axis_index("dom")
    me = lax.axis_index("edge") * n_sub + lax.axis_index("sub")
    width = LANES // inner
    pending = []

    def inner_id(position):
        return {"edge": position // n_sub, "sub": position % n_sub}

    def remote(src, dst, send, recv, where):
        return pltpu.make_async_remote_copy(
            src_ref=src,
            dst_ref=dst,
            send_sem=send,
            recv_sem=recv,
            device_id=where,
            device_id_type=pl.DeviceIdType.MESH,
        )

    def inner_start(pick_src, pick_dst, send, recv):
        copies = []
        for o in range(1, inner):
            target = (me + o) % inner
            copy = remote(
                pick_src(target, o), pick_dst(me, o), send.at[o], recv.at[o], inner_id(target)
            )
            copy.start()
            copies.append(copy)
            pending.append(copy)
        return copies

    def dom_start(src, pick_dst, send, recv):
        copies = []
        for o in range(1, dom):
            target = (my_dom + o) % dom
            copy = remote(src, pick_dst(my_dom, o), send.at[o], recv.at[o], {"dom": target})
            copy.start()
            copies.append(copy)
            pending.append(copy)
        return copies

    def arrive(copies):
        for copy in copies:
            copy.wait_recv()

    def part_slice(position):
        return pl.ds(pl.multiple_of(position * rows, rows), rows)

    def wslice(position):
        return pl.ds(pl.multiple_of(position * width, width), width)

    barrier = pltpu.get_barrier_semaphore()
    for o in range(1, inner):
        pl.semaphore_signal(
            barrier,
            inc=1,
            device_id=inner_id((me + o) % inner),
            device_id_type=pl.DeviceIdType.MESH,
        )
    for o in range(1, dom):
        pl.semaphore_signal(
            barrier,
            inc=1,
            device_id={"dom": (my_dom + o) % dom},
            device_id_type=pl.DeviceIdType.MESH,
        )
    pl.semaphore_wait(barrier, inner - 1 + dom - 1)

    gathered = inner_start(
        lambda target, o: node_lat, lambda mine, o: ext.at[part_slice(mine)], ag_s, ag_r
    )
    ext[part_slice(me), :] = node_lat[...]

    lane = lax.broadcasted_iota(jnp.int32, (LANES, LANES), 1)
    sublane = lax.broadcasted_iota(jnp.int32, (LANES, LANES), 0)

    def columns_of(row):
        return jnp.transpose(jnp.broadcast_to(row, (LANES, LANES)))

    def hot(mask):
        return jnp.where(mask, 1.0, 0.0).astype(BF16)

    for b in range(blocks):
        row = jnp.where(lane[:1] < send_len[0, b], send_idx[b : b + 1, :], -1)
        column = columns_of(row)
        for t in range(0, part_rows, LANES):
            oh_i[b * slot : (b + 1) * slot, t : t + LANES] = hot(column == lane + t)

    for c in range(edges // LANES):
        span = slice(c * LANES, (c + 1) * LANES)
        row_r = receivers[c : c + 1, :]
        column_r = columns_of(row_r)
        for t in range(0, part_rows, LANES):
            oh_r[span, t : t + LANES] = hot(column_r == lane + t)
            oht_r[t : t + LANES, span] = hot(row_r == sublane + t)
        row_s = senders[c : c + 1, :]
        column_s = columns_of(row_s)
        for t in range(0, ext_rows, LANES):
            oh_s[span, t : t + LANES] = hot(column_s == lane + t)
            oht_s[t : t + LANES, span] = hot(row_s == sublane + t)

    arrive(gathered)

    outgoing[...] = nn(oh_i[...], ext[:part_rows, :]).astype(BF16)
    halo = []
    for b in range(blocks):
        target = my_dom + offsets[b]
        source = my_dom - offsets[b]
        has_target = (target >= 0) & (target < dom)
        has_source = (source >= 0) & (source < dom)
        region = ext.at[part_rows + b * slot : part_rows + (b + 1) * slot]
        copy = remote(
            outgoing.at[b * slot : (b + 1) * slot],
            region,
            halo_s.at[b],
            halo_r.at[b],
            {"dom": lax.clamp(0, target, dom - 1)},
        )
        pl.when(has_target)(copy.start)

        @pl.when(jnp.logical_not(has_source))
        def _(region=region):
            region[...] = jnp.zeros(region.shape, BF16)

        halo.append((copy, has_target, has_source))

    proj[part_rows + blocks * slot :, :] = nn(ext[:part_rows, :], edge_w[2]).astype(BF16)
    proj[:part_rows, :] = nn(ext[:part_rows, :], edge_w[1]).astype(BF16)
    for c in range(0, edges, CHUNK):
        span = slice(c, c + CHUNK)
        z1[span, :] = (
            nn(edge_lat[span, :], edge_w[0])
            + nn(oh_r[span, :], proj[ext_rows:, :])
            + nn(oh_s[span, :part_rows], proj[:part_rows, :])
            + edge_b[0:1, :]
        )

    for copy, has_target, has_source in halo:
        pl.when(has_source)(copy.wait_recv)
    proj[part_rows:ext_rows, :] = nn(ext[part_rows:, :], edge_w[1]).astype(BF16)

    for c in range(0, edges, CHUNK):
        span = slice(c, c + CHUNK)
        first = z1[span, :] + nn(oh_s[span, part_rows:], proj[part_rows:ext_rows, :])
        z1[span, :] = first
        act1 = silu(first).astype(BF16)
        a1[span, :] = act1
        second = nn(act1, edge_w[3]) + edge_b[1:2, :]
        z2[span, :] = second
        act2 = silu(second).astype(BF16)
        a2[span, :] = act2
        normed, inv_std = normalise(nn(act2, edge_w[4]) + edge_b[2:3, :])
        normed_e[span, :] = normed
        inv_e[span, :] = inv_std
        valid = lax.broadcasted_iota(jnp.int32, (CHUNK, 1), 0) + c < edge_count[0, 0]
        low_y[span, :] = jnp.where(valid, normed * edge_g[...] + edge_s[...], 0.0).astype(BF16)

    own_acc[...] = nn(oht_r[...], low_y[...])
    sum_send[...] = own_acc[...].astype(BF16)
    summing = inner_start(
        lambda target, o: sum_send.at[part_slice(target)],
        lambda mine, o: sum_recv.at[o],
        sum_s,
        sum_r,
    )

    z1[...] = slope_of(z1[...])
    z2[...] = slope_of(z2[...])
    node_base = nn(node_lat[...], node_w[0]) + node_b[0:1, :]
    cot_n = node_cot[...].astype(F32)

    arrive(summing)
    total = own_acc[part_slice(me), :]
    for o in range(1, inner):
        total = total + sum_recv[o].astype(F32)
    total_low = total.astype(BF16)

    pre1 = node_base + nn(total_low, node_w[1])
    n1 = silu(pre1).astype(BF16)
    pre2 = nn(n1, node_w[2]) + node_b[1:2, :]
    n2 = silu(pre2).astype(BF16)
    normed_n, inv_n = normalise(nn(n2, node_w[3]) + node_b[2:3, :])
    g3 = norm_backward(cot_n * node_g[...], normed_n, inv_n)
    g3_low = g3.astype(BF16)
    g2 = nt(g3_low, node_w[3]) * slope_of(pre2)
    g2_low = g2.astype(BF16)
    g1 = nt(g2_low, node_w[2]) * slope_of(pre1)
    g1_low = g1.astype(BF16)
    agg_own[...] = nt(g1_low, node_w[1]).astype(BF16)
    aggregating = inner_start(
        lambda target, o: agg_own, lambda mine, o: agg.at[part_slice(mine)], agg_s, agg_r
    )
    agg[part_slice(me), :] = agg_own[...]

    out_nodes[...] = cot_n + nt(g1_low, node_w[0])
    nw_stage[0] = tn(node_lat[...], g1_low).astype(BF16)
    nw_stage[1] = tn(total_low, g1_low).astype(BF16)
    nw_stage[2] = tn(n1, g2_low).astype(BF16)
    nw_stage[3] = tn(n2, g3_low).astype(BF16)
    vec[8:9, :] = column_sum(g1)
    vec[9:10, :] = column_sum(g2)
    vec[10:11, :] = column_sum(g3)
    vec[11:12, :] = column_sum(cot_n * normed_n)
    vec[12:16, :] = jnp.zeros((4, LANES), F32)
    vec[5:8, :] = jnp.zeros((3, LANES), F32)

    def reduce_start(stage, recv, send, got):
        return inner_start(
            lambda target, o: stage.at[:, wslice(target), :],
            lambda mine, o: recv.at[o],
            send,
            got,
        )

    def reduce_finish(stage, recv, zown, z, send, got):
        partial = stage[:, wslice(me), :].astype(F32)
        for o in range(1, inner):
            partial = partial + recv[o].astype(F32)
        partial = partial.astype(BF16)
        zown[...] = partial
        z[my_dom] = partial
        return dom_start(zown, lambda mine, o: z.at[mine], send, got)

    def gather_start(z, fown, full, send, got):
        partial = z[0].astype(F32)
        for d in range(1, dom):
            partial = partial + z[d].astype(F32)
        partial = partial.astype(BF16)
        fown[...] = partial
        full[:, wslice(me), :] = partial
        return inner_start(
            lambda target, o: fown, lambda mine, o: full.at[:, wslice(mine), :], send, got
        )

    node_rs = reduce_start(nw_stage, nw_recv, nrs_s, nrs_r)

    arrive(aggregating)
    sums = [jnp.zeros((1, LANES), F32) for _ in range(5)]
    for c in range(0, edges, CHUNK):
        span = slice(c, c + CHUNK)
        valid = lax.broadcasted_iota(jnp.int32, (CHUNK, 1), 0) + c < edge_count[0, 0]
        cot = edge_cot[span, :].astype(F32)
        dy = jnp.where(valid, cot + nn(oh_r[span, :], agg[...]), 0.0)
        normed = normed_e[span, :]
        h3 = norm_backward(dy * edge_g[...], normed, inv_e[span, :])
        h3_low = h3.astype(BF16)
        d3[span, :] = h3_low
        h2 = nt(h3_low, edge_w[4]) * z2[span, :]
        h2_low = h2.astype(BF16)
        d2[span, :] = h2_low
        h1 = nt(h2_low, edge_w[3]) * z1[span, :]
        h1_low = h1.astype(BF16)
        d1[span, :] = h1_low
        out_edges[span, :] = (cot + nt(h1_low, edge_w[0])).astype(BF16)
        for position, term in enumerate((h1, h2, h3, dy * normed, dy)):
            sums[position] = sums[position] + column_sum(term)

    for position in range(5):
        vec[position : position + 1, :] = sums[position]
    vec_in[me] = vec[...]
    vec_rs = inner_start(lambda target, o: vec, lambda mine, o: vec_in.at[mine], vrs_s, vrs_r)

    back_send[...] = nn(oht_s[part_rows:, :], d1[...]).astype(BF16)
    returning = []
    for b in range(blocks):
        target = my_dom - offsets[b]
        source = my_dom + offsets[b]
        has_target = (target >= 0) & (target < dom)
        has_source = (source >= 0) & (source < dom)
        region = back_recv.at[b * slot : (b + 1) * slot]
        copy = remote(
            back_send.at[b * slot : (b + 1) * slot],
            region,
            back_s.at[b],
            back_r.at[b],
            {"dom": lax.clamp(0, target, dom - 1)},
        )
        pl.when(has_target)(copy.start)

        @pl.when(jnp.logical_not(has_source))
        def _(region=region):
            region[...] = jnp.zeros(region.shape, BF16)

        returning.append((copy, has_target, has_source))

    own_low = nn(oht_s[:part_rows, :], d1[...]).astype(BF16)
    recv_low = nn(oht_r[...], d1[...]).astype(BF16)
    ew_stage[0] = tn(edge_lat[...], d1[...]).astype(BF16)
    ew_stage[1] = (tn(ext[:part_rows, :], own_low) + tn(ext[part_rows:, :], back_send[...])).astype(
        BF16
    )
    ew_stage[2] = tn(ext[:part_rows, :], recv_low).astype(BF16)
    ew_stage[3] = tn(a1[...], d2[...]).astype(BF16)
    ew_stage[4] = tn(a2[...], d3[...]).astype(BF16)
    edge_rs = reduce_start(ew_stage, ew_recv, ers_s, ers_r)
    own_acc[...] = nt(own_low, edge_w[1]) + nt(recv_low, edge_w[2])

    arrive(node_rs)
    node_z = reduce_finish(nw_stage, nw_recv, nw_zown, nw_z, nz_s, nz_r)

    for copy, has_target, has_source in returning:
        pl.when(has_source)(copy.wait_recv)
    scattered = tn(oh_i[...], back_recv[...]).astype(BF16)
    own_acc[...] = own_acc[...] + nt(scattered, edge_w[1])
    own_send[...] = own_acc[...].astype(BF16)
    owning = inner_start(
        lambda target, o: own_send.at[part_slice(target)],
        lambda mine, o: own_recv.at[o],
        own_s,
        own_r,
    )

    arrive(edge_rs)
    edge_z = reduce_finish(ew_stage, ew_recv, ew_zown, ew_z, ez_s, ez_r)
    arrive(vec_rs)
    vec_sum = vec_in[0]
    for position in range(1, inner):
        vec_sum = vec_sum + vec_in[position]
    vec_zown[...] = vec_sum
    vec_z[my_dom] = vec_sum
    vec_all = dom_start(vec_zown, lambda mine, o: vec_z.at[mine], vz_s, vz_r)

    arrive(node_z)
    node_ag = gather_start(nw_z, nw_fown, nw_full, nag_s, nag_r)

    arrive(owning)
    mine = own_acc[part_slice(me), :]
    for o in range(1, inner):
        mine = mine + own_recv[o].astype(F32)
    out_nodes[...] = out_nodes[...] + mine

    arrive(edge_z)
    edge_ag = gather_start(ew_z, ew_fown, ew_full, eag_s, eag_r)

    edge_scale = 1.0 / math.sqrt(edges * dom * inner)
    node_scale = 1.0 / math.sqrt(rows * dom * inner)
    arrive(vec_all)
    vec_sum = vec_z[0]
    for d in range(1, dom):
        vec_sum = vec_sum + vec_z[d]
    out_ev[...] = vec_sum[0:5, :] * edge_scale
    out_nv[...] = vec_sum[8:12, :] * node_scale
    arrive(node_ag)
    out_nw[...] = nw_full[...].astype(F32) * node_scale
    arrive(edge_ag)
    out_ew[...] = ew_full[...].astype(F32) * edge_scale

    for copy in pending:
        copy.wait_send()
    for copy, has_target, has_source in halo + returning:
        pl.when(has_target)(copy.wait_send)


def local(sizes, *arrays):
    (
        node_lat,
        edge_lat,
        node_cot,
        edge_cot,
        senders,
        receivers,
        send_idx,
        send_len,
        edge_count,
        edge_w,
        edge_b,
        edge_g,
        edge_s,
        node_w,
        node_b,
        node_g,
    ) = arrays
    dom, n_edge, n_sub = sizes
    inner = n_edge * n_sub
    rows, features = node_lat.shape
    edges = edge_lat.shape[0]
    blocks, slot = send_idx.shape[1:]
    part_rows = rows * inner
    ext_rows = part_rows + blocks * slot
    width = features // inner
    operands = (
        node_lat,
        edge_lat,
        node_cot,
        edge_cot,
        senders.reshape(edges // LANES, LANES),
        receivers.reshape(edges // LANES, LANES),
        send_idx[0],
        send_len,
        edge_count,
        edge_w,
        edge_b,
        edge_g.reshape(1, features),
        edge_s.reshape(1, features),
        node_w,
        node_b,
        node_g.reshape(1, features),
    )
    vmem = pl.BlockSpec(memory_space=pltpu.VMEM)
    smem = pl.BlockSpec(memory_space=pltpu.SMEM)
    in_specs = [smem if position in (7, 8) else vmem for position in range(len(operands))]

    def low(*shape):
        return pltpu.VMEM(shape + (features,), BF16)

    def full(*shape):
        return pltpu.VMEM(shape + (features,), F32)

    def weights(count):
        return [
            low(count, features),
            low(inner, count, width),
            low(count, width),
            low(dom, count, width),
            low(count, width),
            low(count, features),
        ]

    def sems(count):
        return [pltpu.SemaphoreType.DMA((count,)), pltpu.SemaphoreType.DMA((count,))]

    scratch = [
        low(ext_rows),
        low(blocks * slot),
        pltpu.VMEM((edges, ext_rows), BF16),
        pltpu.VMEM((ext_rows, edges), BF16),
        pltpu.VMEM((edges, part_rows), BF16),
        pltpu.VMEM((part_rows, edges), BF16),
        pltpu.VMEM((blocks * slot, part_rows), BF16),
        low(ext_rows + part_rows),
        full(edges),
        full(edges),
        low(edges),
        low(edges),
        full(edges),
        pltpu.VMEM((edges, 1), F32),
        low(edges),
        low(part_rows),
        low(inner, rows),
        low(part_rows),
        low(rows),
        low(edges),
        low(edges),
        low(edges),
        low(blocks * slot),
        low(blocks * slot),
        full(part_rows),
        low(part_rows),
        low(inner, rows),
        *weights(4),
        *weights(5),
        full(16),
        full(inner, 16),
        full(16),
        full(dom, 16),
        *sems(inner),
        *sems(blocks),
        *sems(inner),
        *sems(inner),
        *sems(blocks),
        *sems(inner),
        *sems(inner),
        *sems(dom),
        *sems(inner),
        *sems(inner),
        *sems(dom),
        *sems(inner),
        *sems(inner),
        *sems(dom),
    ]
    return pl.pallas_call(
        functools.partial(kernel, sizes),
        out_shape=(
            jax.ShapeDtypeStruct((rows, features), F32),
            jax.ShapeDtypeStruct((edges, features), BF16),
            jax.ShapeDtypeStruct((5, features, features), F32),
            jax.ShapeDtypeStruct((5, features), F32),
            jax.ShapeDtypeStruct((4, features, features), F32),
            jax.ShapeDtypeStruct((4, features), F32),
        ),
        in_specs=in_specs,
        out_specs=(vmem,) * 6,
        scratch_shapes=scratch,
        compiler_params=pltpu.CompilerParams(
            collective_id=0, has_side_effects=True, vmem_limit_bytes=48 * 1024 * 1024
        ),
    )(*operands)


def solution(mesh):
    sizes = (mesh.shape["dom"], mesh.shape["edge"], mesh.shape["sub"])
    part = P(("groups", "dom", "edge", "sub"), None)
    index = P(("groups", "dom", "edge", "sub"))
    return jax.shard_map(
        functools.partial(local, sizes),
        mesh=mesh,
        in_specs=(
            part,
            part,
            part,
            part,
            index,
            index,
            P(("groups", "dom"), None, None),
            P(("groups", "dom"), None),
            P(("groups", "dom"), ("edge", "sub")),
        )
        + (P(),) * 7,
        out_specs=(
            part,
            part,
            P("groups", None, None),
            P("groups", None),
            P("groups", None, None),
            P("groups", None),
        ),
        check_vma=False,
    )
```

```python
import functools
import math

import jax
import jax.numpy as jnp
from jax import lax
from jax.experimental import pallas as pl
from jax.experimental.pallas import tpu as pltpu
from jax.sharding import PartitionSpec as P

EPSILON = 1e-05
F32 = jnp.float32
BF16 = jnp.bfloat16
LANES = 128
CHUNK = 256
VMEM_BYTES = 63 * 1024 * 1024


def nn(left, right):
    return lax.dot_general(left, right, (((1,), (0,)), ((), ())), preferred_element_type=F32)


def nt(left, right):
    return lax.dot_general(left, right, (((1,), (1,)), ((), ())), preferred_element_type=F32)


def tn(left, right):
    return lax.dot_general(left, right, (((0,), (0,)), ((), ())), preferred_element_type=F32)


def sigmoid(values):
    return 0.5 * jnp.tanh(0.5 * values) + 0.5


def slope_of(values):
    gate = sigmoid(values)
    return gate * (1.0 + values * (1.0 - gate))


def silu(values):
    return values * sigmoid(values)


def normalise(pre):
    centred = pre - jnp.mean(pre, axis=1, keepdims=True)
    inv_std = lax.rsqrt(jnp.mean(centred * centred, axis=1, keepdims=True) + EPSILON)
    return centred * inv_std, inv_std


def norm_backward(scaled, normed, inv_std):
    return inv_std * (
        scaled
        - jnp.mean(scaled, axis=1, keepdims=True)
        - normed * jnp.mean(scaled * normed, axis=1, keepdims=True)
    )


def column_sum(values):
    return jnp.sum(values, axis=0, keepdims=True)


def kernel(
    sizes,
    hbm_node_lat,
    hbm_edge_lat,
    hbm_node_cot,
    hbm_edge_cot,
    hbm_senders,
    hbm_receivers,
    hbm_send_idx,
    hbm_send_len,
    hbm_edge_count,
    hbm_edge_w,
    hbm_edge_b,
    hbm_edge_g,
    hbm_edge_s,
    hbm_node_w,
    hbm_node_b,
    hbm_node_g,
    hbm_out_nodes,
    hbm_out_edges,
    hbm_out_ew,
    hbm_out_nw,
    hbm_out_vec,
    out_nodes,
    out_edges,
    out_ew,
    out_nw,
    out_vec,
    store_sem,
    node_lat,
    edge_lat,
    node_cot,
    edge_cot,
    senders,
    receivers,
    send_idx,
    send_len,
    edge_count,
    edge_w,
    edge_b,
    edge_g,
    edge_s,
    node_w,
    node_b,
    node_g,
    load_sem,
    ext,
    outgoing,
    oh_s,
    oht_s,
    oh_r,
    oht_r,
    oh_i,
    proj,
    z1,
    z2,
    a1,
    a2,
    normed_e,
    inv_e,
    low_y,
    sum_send,
    sum_recv,
    agg,
    agg_own,
    d1,
    d2,
    d3,
    back_send,
    back_recv,
    own_acc,
    own_send,
    own_recv,
    nw_stage,
    nw_recv,
    nw_zown,
    nw_z,
    nw_fown,
    nw_full,
    ew_stage,
    ew_recv,
    ew_zown,
    ew_z,
    ew_fown,
    ew_full,
    vec,
    vec_in,
    vec_zown,
    vec_z,
    ag_s,
    ag_r,
    halo_s,
    halo_r,
    sum_s,
    sum_r,
    agg_s,
    agg_r,
    back_s,
    back_r,
    own_s,
    own_r,
    nrs_s,
    nrs_r,
    nz_s,
    nz_r,
    nag_s,
    nag_r,
    ers_s,
    ers_r,
    ez_s,
    ez_r,
    eag_s,
    eag_r,
    vrs_s,
    vrs_r,
    vz_s,
    vz_r,
):
    loads = {}
    for name, src, dst in (
        ("node_lat", hbm_node_lat, node_lat),
        ("edge_lat", hbm_edge_lat, edge_lat),
        ("node_cot", hbm_node_cot, node_cot),
        ("edge_cot", hbm_edge_cot, edge_cot),
        ("senders", hbm_senders, senders),
        ("receivers", hbm_receivers, receivers),
        ("send_idx", hbm_send_idx, send_idx),
        ("send_len", hbm_send_len, send_len),
        ("edge_count", hbm_edge_count, edge_count),
        ("edge_w", hbm_edge_w, edge_w),
        ("edge_b", hbm_edge_b, edge_b),
        ("edge_g", hbm_edge_g, edge_g),
        ("edge_s", hbm_edge_s, edge_s),
        ("node_w", hbm_node_w, node_w),
        ("node_b", hbm_node_b, node_b),
        ("node_g", hbm_node_g, node_g),
    ):
        loads[name] = pltpu.make_async_copy(src, dst, load_sem.at[len(loads)])
        loads[name].start()

    stores = []

    def store(src, dst):
        stores.append(pltpu.make_async_copy(src, dst, store_sem.at[len(stores)]))
        stores[-1].start()

    def ready(*wanted):
        for name in wanted:
            loads[name].wait()

    dom, n_edge, n_sub = sizes
    inner = n_edge * n_sub
    rows = node_lat.shape[0]
    edges = edge_lat.shape[0]
    part_rows = rows * inner
    blocks, slot = send_idx.shape
    ext_rows = part_rows + blocks * slot
    reach = blocks // 2
    offsets = [b - reach if b < reach else b - reach + 1 for b in range(blocks)]
    my_dom = lax.axis_index("dom")
    me = lax.axis_index("edge") * n_sub + lax.axis_index("sub")
    width = LANES // inner
    pending = []

    def inner_id(position):
        return {"edge": position // n_sub, "sub": position % n_sub}

    def remote(src, dst, send, recv, where):
        return pltpu.make_async_remote_copy(
            src_ref=src,
            dst_ref=dst,
            send_sem=send,
            recv_sem=recv,
            device_id=where,
            device_id_type=pl.DeviceIdType.MESH,
        )

    def inner_start(pick_src, pick_dst, send, recv):
        copies = []
        for o in range(1, inner):
            target = (me + o) % inner
            copy = remote(
                pick_src(target, o), pick_dst(me, o), send.at[o], recv.at[o], inner_id(target)
            )
            copy.start()
            copies.append(copy)
            pending.append(copy)
        return copies

    def dom_start(src, pick_dst, send, recv):
        copies = []
        for o in range(1, dom):
            target = (my_dom + o) % dom
            copy = remote(src, pick_dst(my_dom, o), send.at[o], recv.at[o], {"dom": target})
            copy.start()
            copies.append(copy)
            pending.append(copy)
        return copies

    def arrive(copies):
        for copy in copies:
            copy.wait_recv()

    def part_slice(position):
        return pl.ds(pl.multiple_of(position * rows, rows), rows)

    def wslice(position):
        return pl.ds(pl.multiple_of(position * width, width), width)

    barrier = pltpu.get_barrier_semaphore()
    for o in range(1, inner):
        pl.semaphore_signal(
            barrier,
            inc=1,
            device_id=inner_id((me + o) % inner),
            device_id_type=pl.DeviceIdType.MESH,
        )
    for o in range(1, dom):
        pl.semaphore_signal(
            barrier,
            inc=1,
            device_id={"dom": (my_dom + o) % dom},
            device_id_type=pl.DeviceIdType.MESH,
        )
    pl.semaphore_wait(barrier, inner - 1 + dom - 1)

    ready("node_lat")
    gathered = inner_start(
        lambda target, o: node_lat, lambda mine, o: ext.at[part_slice(mine)], ag_s, ag_r
    )
    ext[part_slice(me), :] = node_lat[...]

    lane = lax.broadcasted_iota(jnp.int32, (LANES, LANES), 1)
    sublane = lax.broadcasted_iota(jnp.int32, (LANES, LANES), 0)

    ready("send_idx", "send_len", "senders", "receivers")

    def columns_of(row):
        return jnp.transpose(jnp.broadcast_to(row, (LANES, LANES)))

    def hot(mask):
        return jnp.where(mask, 1.0, 0.0).astype(BF16)

    for b in range(blocks):
        row = jnp.where(lane[:1] < send_len[:, b : b + 1], send_idx[b : b + 1, :], -1)
        column = columns_of(row)
        for t in range(0, part_rows, LANES):
            oh_i[b * slot : (b + 1) * slot, t : t + LANES] = hot(column == lane + t)

    for c in range(edges // LANES):
        span = slice(c * LANES, (c + 1) * LANES)
        row_r = receivers[c : c + 1, :]
        column_r = columns_of(row_r)
        for t in range(0, part_rows, LANES):
            oh_r[span, t : t + LANES] = hot(column_r == lane + t)
            oht_r[t : t + LANES, span] = hot(row_r == sublane + t)
        row_s = senders[c : c + 1, :]
        column_s = columns_of(row_s)
        for t in range(0, ext_rows, LANES):
            oh_s[span, t : t + LANES] = hot(column_s == lane + t)
            oht_s[t : t + LANES, span] = hot(row_s == sublane + t)

    ready(
        "edge_lat", "edge_cot", "edge_count", "edge_w", "edge_b", "edge_g", "edge_s",
        "node_cot", "node_w", "node_b", "node_g",
    )
    arrive(gathered)

    outgoing[...] = nn(oh_i[...], ext[:part_rows, :]).astype(BF16)
    halo = []
    for b in range(blocks):
        target = my_dom + offsets[b]
        source = my_dom - offsets[b]
        has_target = (target >= 0) & (target < dom)
        has_source = (source >= 0) & (source < dom)
        region = ext.at[part_rows + b * slot : part_rows + (b + 1) * slot]
        copy = remote(
            outgoing.at[b * slot : (b + 1) * slot],
            region,
            halo_s.at[b],
            halo_r.at[b],
            {"dom": lax.clamp(0, target, dom - 1)},
        )
        pl.when(has_target)(copy.start)

        @pl.when(jnp.logical_not(has_source))
        def _(region=region):
            region[...] = jnp.zeros(region.shape, BF16)

        halo.append((copy, has_target, has_source))

    proj[part_rows + blocks * slot :, :] = nn(ext[:part_rows, :], edge_w[2]).astype(BF16)
    proj[:part_rows, :] = nn(ext[:part_rows, :], edge_w[1]).astype(BF16)
    for c in range(0, edges, CHUNK):
        span = slice(c, c + CHUNK)
        z1[span, :] = (
            nn(edge_lat[span, :], edge_w[0])
            + nn(oh_r[span, :], proj[ext_rows:, :])
            + nn(oh_s[span, :part_rows], proj[:part_rows, :])
            + edge_b[0:1, :]
        )

    for copy, has_target, has_source in halo:
        pl.when(has_source)(copy.wait_recv)
    proj[part_rows:ext_rows, :] = nn(ext[part_rows:, :], edge_w[1]).astype(BF16)

    for c in range(0, edges, CHUNK):
        span = slice(c, c + CHUNK)
        first = z1[span, :] + nn(oh_s[span, part_rows:], proj[part_rows:ext_rows, :])
        z1[span, :] = first
        act1 = silu(first).astype(BF16)
        a1[span, :] = act1
        second = nn(act1, edge_w[3]) + edge_b[1:2, :]
        z2[span, :] = second
        act2 = silu(second).astype(BF16)
        a2[span, :] = act2
        normed, inv_std = normalise(nn(act2, edge_w[4]) + edge_b[2:3, :])
        normed_e[span, :] = normed
        inv_e[span, :] = inv_std
        valid = lax.broadcasted_iota(jnp.int32, (CHUNK, 1), 0) + c < edge_count[...]
        low_y[span, :] = jnp.where(valid, normed * edge_g[...] + edge_s[...], 0.0).astype(BF16)

    own_acc[...] = nn(oht_r[...], low_y[...])
    sum_send[...] = own_acc[...].astype(BF16)
    summing = inner_start(
        lambda target, o: sum_send.at[part_slice(target)],
        lambda mine, o: sum_recv.at[o],
        sum_s,
        sum_r,
    )

    z1[...] = slope_of(z1[...])
    z2[...] = slope_of(z2[...])
    node_base = nn(node_lat[...], node_w[0]) + node_b[0:1, :]
    cot_n = node_cot[...].astype(F32)

    arrive(summing)
    total = own_acc[part_slice(me), :]
    for o in range(1, inner):
        total = total + sum_recv[o].astype(F32)
    total_low = total.astype(BF16)

    pre1 = node_base + nn(total_low, node_w[1])
    n1 = silu(pre1).astype(BF16)
    pre2 = nn(n1, node_w[2]) + node_b[1:2, :]
    n2 = silu(pre2).astype(BF16)
    normed_n, inv_n = normalise(nn(n2, node_w[3]) + node_b[2:3, :])
    g3 = norm_backward(cot_n * node_g[...], normed_n, inv_n)
    g3_low = g3.astype(BF16)
    g2 = nt(g3_low, node_w[3]) * slope_of(pre2)
    g2_low = g2.astype(BF16)
    g1 = nt(g2_low, node_w[2]) * slope_of(pre1)
    g1_low = g1.astype(BF16)
    agg_own[...] = nt(g1_low, node_w[1]).astype(BF16)
    aggregating = inner_start(
        lambda target, o: agg_own, lambda mine, o: agg.at[part_slice(mine)], agg_s, agg_r
    )
    agg[part_slice(me), :] = agg_own[...]

    out_nodes[...] = cot_n + nt(g1_low, node_w[0])
    nw_stage[0] = tn(node_lat[...], g1_low).astype(BF16)
    nw_stage[1] = tn(total_low, g1_low).astype(BF16)
    nw_stage[2] = tn(n1, g2_low).astype(BF16)
    nw_stage[3] = tn(n2, g3_low).astype(BF16)
    vec[8:9, :] = column_sum(g1)
    vec[9:10, :] = column_sum(g2)
    vec[10:11, :] = column_sum(g3)
    vec[11:12, :] = column_sum(cot_n * normed_n)
    vec[12:16, :] = jnp.zeros((4, LANES), F32)
    vec[5:8, :] = jnp.zeros((3, LANES), F32)

    def reduce_start(stage, recv, send, got):
        return inner_start(
            lambda target, o: stage.at[:, wslice(target), :],
            lambda mine, o: recv.at[o],
            send,
            got,
        )

    def reduce_finish(stage, recv, zown, z, send, got):
        partial = stage[:, wslice(me), :].astype(F32)
        for o in range(1, inner):
            partial = partial + recv[o].astype(F32)
        partial = partial.astype(BF16)
        zown[...] = partial
        z[my_dom] = partial
        return dom_start(zown, lambda mine, o: z.at[mine], send, got)

    def gather_start(z, fown, full, send, got):
        partial = z[0].astype(F32)
        for d in range(1, dom):
            partial = partial + z[d].astype(F32)
        partial = partial.astype(BF16)
        fown[...] = partial
        full[:, wslice(me), :] = partial
        return inner_start(
            lambda target, o: fown, lambda mine, o: full.at[:, wslice(mine), :], send, got
        )

    node_rs = reduce_start(nw_stage, nw_recv, nrs_s, nrs_r)

    arrive(aggregating)
    sums = [jnp.zeros((1, LANES), F32) for _ in range(5)]
    for c in range(0, edges, CHUNK):
        span = slice(c, c + CHUNK)
        valid = lax.broadcasted_iota(jnp.int32, (CHUNK, 1), 0) + c < edge_count[...]
        cot = edge_cot[span, :].astype(F32)
        dy = jnp.where(valid, cot + nn(oh_r[span, :], agg[...]), 0.0)
        normed = normed_e[span, :]
        h3 = norm_backward(dy * edge_g[...], normed, inv_e[span, :])
        h3_low = h3.astype(BF16)
        d3[span, :] = h3_low
        h2 = nt(h3_low, edge_w[4]) * z2[span, :]
        h2_low = h2.astype(BF16)
        d2[span, :] = h2_low
        h1 = nt(h2_low, edge_w[3]) * z1[span, :]
        h1_low = h1.astype(BF16)
        d1[span, :] = h1_low
        out_edges[span, :] = (cot + nt(h1_low, edge_w[0])).astype(BF16)
        for position, term in enumerate((h1, h2, h3, dy * normed, dy)):
            sums[position] = sums[position] + column_sum(term)

    store(out_edges, hbm_out_edges)
    for position in range(5):
        vec[position : position + 1, :] = sums[position]
    vec_in[me] = vec[...]
    vec_rs = inner_start(lambda target, o: vec, lambda mine, o: vec_in.at[mine], vrs_s, vrs_r)

    back_send[...] = nn(oht_s[part_rows:, :], d1[...]).astype(BF16)
    returning = []
    for b in range(blocks):
        target = my_dom - offsets[b]
        source = my_dom + offsets[b]
        has_target = (target >= 0) & (target < dom)
        has_source = (source >= 0) & (source < dom)
        region = back_recv.at[b * slot : (b + 1) * slot]
        copy = remote(
            back_send.at[b * slot : (b + 1) * slot],
            region,
            back_s.at[b],
            back_r.at[b],
            {"dom": lax.clamp(0, target, dom - 1)},
        )
        pl.when(has_target)(copy.start)

        @pl.when(jnp.logical_not(has_source))
        def _(region=region):
            region[...] = jnp.zeros(region.shape, BF16)

        returning.append((copy, has_target, has_source))

    own_low = nn(oht_s[:part_rows, :], d1[...]).astype(BF16)
    recv_low = nn(oht_r[...], d1[...]).astype(BF16)
    ew_stage[0] = tn(edge_lat[...], d1[...]).astype(BF16)
    ew_stage[1] = (tn(ext[:part_rows, :], own_low) + tn(ext[part_rows:, :], back_send[...])).astype(
        BF16
    )
    ew_stage[2] = tn(ext[:part_rows, :], recv_low).astype(BF16)
    ew_stage[3] = tn(a1[...], d2[...]).astype(BF16)
    ew_stage[4] = tn(a2[...], d3[...]).astype(BF16)
    edge_rs = reduce_start(ew_stage, ew_recv, ers_s, ers_r)
    own_acc[...] = nt(own_low, edge_w[1]) + nt(recv_low, edge_w[2])

    arrive(node_rs)
    node_z = reduce_finish(nw_stage, nw_recv, nw_zown, nw_z, nz_s, nz_r)

    for copy, has_target, has_source in returning:
        pl.when(has_source)(copy.wait_recv)
    scattered = tn(oh_i[...], back_recv[...]).astype(BF16)
    own_acc[...] = own_acc[...] + nt(scattered, edge_w[1])
    own_send[...] = own_acc[...].astype(BF16)
    owning = inner_start(
        lambda target, o: own_send.at[part_slice(target)],
        lambda mine, o: own_recv.at[o],
        own_s,
        own_r,
    )

    arrive(edge_rs)
    edge_z = reduce_finish(ew_stage, ew_recv, ew_zown, ew_z, ez_s, ez_r)
    arrive(vec_rs)
    vec_sum = vec_in[0]
    for position in range(1, inner):
        vec_sum = vec_sum + vec_in[position]
    vec_zown[...] = vec_sum
    vec_z[my_dom] = vec_sum
    vec_all = dom_start(vec_zown, lambda mine, o: vec_z.at[mine], vz_s, vz_r)

    arrive(node_z)
    node_ag = gather_start(nw_z, nw_fown, nw_full, nag_s, nag_r)

    arrive(owning)
    mine = own_acc[part_slice(me), :]
    for o in range(1, inner):
        mine = mine + own_recv[o].astype(F32)
    out_nodes[...] = out_nodes[...] + mine
    store(out_nodes, hbm_out_nodes)

    arrive(edge_z)
    edge_ag = gather_start(ew_z, ew_fown, ew_full, eag_s, eag_r)

    edge_scale = 1.0 / math.sqrt(edges * dom * inner)
    node_scale = 1.0 / math.sqrt(rows * dom * inner)
    arrive(vec_all)
    vec_sum = vec_z[0]
    for d in range(1, dom):
        vec_sum = vec_sum + vec_z[d]
    out_vec[0:8, :] = vec_sum[0:8, :] * edge_scale
    out_vec[8:16, :] = vec_sum[8:16, :] * node_scale
    store(out_vec, hbm_out_vec)
    arrive(node_ag)
    out_nw[...] = nw_full[...].astype(F32) * node_scale
    store(out_nw, hbm_out_nw)
    arrive(edge_ag)
    out_ew[...] = ew_full[...].astype(F32) * edge_scale
    store(out_ew, hbm_out_ew)

    for copy in stores:
        copy.wait()
    for copy in pending:
        copy.wait_send()
    for copy, has_target, has_source in halo + returning:
        pl.when(has_target)(copy.wait_send)


def store_kernel(
    nodes,
    edges,
    ew,
    nw,
    vec,
    out_nodes,
    out_edges,
    out_ew,
    out_ev,
    out_nw,
    out_nv,
    v_nodes,
    v_edges,
    v_ew,
    v_nw,
    v_ev,
    v_nv,
    load_sem,
    store_sem,
):
    routes = (
        (vec.at[0:5], v_ev, out_ev),
        (vec.at[8:12], v_nv, out_nv),
        (nodes, v_nodes, out_nodes),
        (edges, v_edges, out_edges),
        (nw, v_nw, out_nw),
        (ew, v_ew, out_ew),
    )
    loads = [
        pltpu.make_async_copy(src, mid, load_sem.at[position])
        for position, (src, mid, _) in enumerate(routes)
    ]
    stores = [
        pltpu.make_async_copy(mid, dst, store_sem.at[position])
        for position, (_, mid, dst) in enumerate(routes)
    ]
    for copy in loads:
        copy.start()
    for load, copy in zip(loads, stores):
        load.wait()
        copy.start()
    for copy in stores:
        copy.wait()


def local(sizes, *arrays):
    (
        node_lat,
        edge_lat,
        node_cot,
        edge_cot,
        senders,
        receivers,
        send_idx,
        send_len,
        edge_count,
        edge_w,
        edge_b,
        edge_g,
        edge_s,
        node_w,
        node_b,
        node_g,
    ) = arrays
    dom, n_edge, n_sub = sizes
    inner = n_edge * n_sub
    rows, features = node_lat.shape
    edges = edge_lat.shape[0]
    blocks, slot = send_idx.shape[1:]
    part_rows = rows * inner
    ext_rows = part_rows + blocks * slot
    width = features // inner
    operands = (
        node_lat,
        edge_lat,
        node_cot,
        edge_cot,
        senders.reshape(edges // LANES, LANES),
        receivers.reshape(edges // LANES, LANES),
        send_idx[0],
        send_len,
        edge_count,
        edge_w,
        edge_b,
        edge_g.reshape(1, features),
        edge_s.reshape(1, features),
        node_w,
        node_b,
        node_g.reshape(1, features),
    )
    hbm = pl.BlockSpec(memory_space=pltpu.HBM)

    def low(*shape):
        return pltpu.VMEM(shape + (features,), BF16)

    def full(*shape):
        return pltpu.VMEM(shape + (features,), F32)

    def weights(count):
        return [
            low(count, features),
            low(inner, count, width),
            low(count, width),
            low(dom, count, width),
            low(count, width),
            low(count, features),
        ]

    def sems(count):
        return [pltpu.SemaphoreType.DMA((count,)), pltpu.SemaphoreType.DMA((count,))]

    scratch = [
        full(rows),
        low(edges),
        full(5, features),
        full(4, features),
        full(16),
        pltpu.SemaphoreType.DMA((5,)),
        *[pltpu.VMEM(array.shape, array.dtype) for array in operands],
        pltpu.SemaphoreType.DMA((len(operands),)),
        low(ext_rows),
        low(blocks * slot),
        pltpu.VMEM((edges, ext_rows), BF16),
        pltpu.VMEM((ext_rows, edges), BF16),
        pltpu.VMEM((edges, part_rows), BF16),
        pltpu.VMEM((part_rows, edges), BF16),
        pltpu.VMEM((blocks * slot, part_rows), BF16),
        low(ext_rows + part_rows),
        full(edges),
        full(edges),
        low(edges),
        low(edges),
        full(edges),
        pltpu.VMEM((edges, 1), F32),
        low(edges),
        low(part_rows),
        low(inner, rows),
        low(part_rows),
        low(rows),
        low(edges),
        low(edges),
        low(edges),
        low(blocks * slot),
        low(blocks * slot),
        full(part_rows),
        low(part_rows),
        low(inner, rows),
        *weights(4),
        *weights(5),
        full(16),
        full(inner, 16),
        full(16),
        full(dom, 16),
        *sems(inner),
        *sems(blocks),
        *sems(inner),
        *sems(inner),
        *sems(blocks),
        *sems(inner),
        *sems(inner),
        *sems(dom),
        *sems(inner),
        *sems(inner),
        *sems(dom),
        *sems(inner),
        *sems(inner),
        *sems(dom),
    ]
    results = pl.pallas_call(
        functools.partial(kernel, sizes),
        out_shape=(
            jax.ShapeDtypeStruct((rows, features), F32),
            jax.ShapeDtypeStruct((edges, features), BF16),
            jax.ShapeDtypeStruct((5, features, features), F32),
            jax.ShapeDtypeStruct((4, features, features), F32),
            jax.ShapeDtypeStruct((16, features), F32),
        ),
        in_specs=[hbm] * len(operands),
        out_specs=(hbm,) * 5,
        scratch_shapes=scratch,
        compiler_params=pltpu.CompilerParams(
            collective_id=0, has_side_effects=True, vmem_limit_bytes=VMEM_BYTES
        ),
    )(*operands)
    return pl.pallas_call(
        store_kernel,
        out_shape=(
            jax.ShapeDtypeStruct((rows, features), F32),
            jax.ShapeDtypeStruct((edges, features), BF16),
            jax.ShapeDtypeStruct((5, features, features), F32),
            jax.ShapeDtypeStruct((5, features), F32),
            jax.ShapeDtypeStruct((4, features, features), F32),
            jax.ShapeDtypeStruct((4, features), F32),
        ),
        in_specs=[hbm] * 5,
        out_specs=(hbm,) * 6,
        scratch_shapes=[
            full(rows),
            low(edges),
            full(5, features),
            full(4, features),
            full(5),
            full(4),
            pltpu.SemaphoreType.DMA((6,)),
            pltpu.SemaphoreType.DMA((6,)),
        ],
        compiler_params=pltpu.CompilerParams(vmem_limit_bytes=VMEM_BYTES),
    )(*results)


def solution(mesh):
    sizes = (mesh.shape["dom"], mesh.shape["edge"], mesh.shape["sub"])
    part = P(("groups", "dom", "edge", "sub"), None)
    index = P(("groups", "dom", "edge", "sub"))
    return jax.shard_map(
        functools.partial(local, sizes),
        mesh=mesh,
        in_specs=(
            part,
            part,
            part,
            part,
            index,
            index,
            P(("groups", "dom"), None, None),
            P(("groups", "dom"), None),
            P(("groups", "dom"), ("edge", "sub")),
        )
        + (P(),) * 7,
        out_specs=(
            part,
            part,
            P("groups", None, None),
            P("groups", None),
            P("groups", None, None),
            P("groups", None),
        ),
        check_vma=False,
    )
```

```python
import functools
import math

import jax
import jax.numpy as jnp
from jax import lax
from jax.experimental import pallas as pl
from jax.experimental.pallas import tpu as pltpu
from jax.sharding import PartitionSpec as P

EPSILON = 1e-05
F32 = jnp.float32
BF16 = jnp.bfloat16
LANES = 128
CHUNK = 256
VMEM_BYTES = 63 * 1024 * 1024


def nn(left, right):
    return lax.dot_general(left, right, (((1,), (0,)), ((), ())), preferred_element_type=F32)


def nt(left, right):
    return lax.dot_general(left, right, (((1,), (1,)), ((), ())), preferred_element_type=F32)


def tn(left, right):
    return lax.dot_general(left, right, (((0,), (0,)), ((), ())), preferred_element_type=F32)


def sigmoid(values):
    return 0.5 * jnp.tanh(0.5 * values) + 0.5


def slope_of(values):
    gate = sigmoid(values)
    return gate * (1.0 + values * (1.0 - gate))


def silu(values):
    return values * sigmoid(values)


def normalise(pre):
    centred = pre - jnp.mean(pre, axis=1, keepdims=True)
    inv_std = lax.rsqrt(jnp.mean(centred * centred, axis=1, keepdims=True) + EPSILON)
    return centred * inv_std, inv_std


def norm_backward(scaled, normed, inv_std):
    return inv_std * (
        scaled
        - jnp.mean(scaled, axis=1, keepdims=True)
        - normed * jnp.mean(scaled * normed, axis=1, keepdims=True)
    )


def column_sum(values):
    return jnp.sum(values, axis=0, keepdims=True)


def kernel(
    sizes,
    hbm_node_lat,
    hbm_edge_lat,
    hbm_node_cot,
    hbm_edge_cot,
    hbm_senders,
    hbm_receivers,
    hbm_send_idx,
    hbm_send_len,
    hbm_edge_count,
    hbm_edge_w,
    hbm_edge_b,
    hbm_edge_g,
    hbm_edge_s,
    hbm_node_w,
    hbm_node_b,
    hbm_node_g,
    hbm_out_nodes,
    hbm_out_edges,
    hbm_out_ew,
    hbm_out_nw,
    hbm_out_vec,
    out_nodes,
    out_edges,
    out_ew,
    out_nw,
    out_vec,
    store_sem,
    node_lat,
    edge_lat,
    node_cot,
    edge_cot,
    senders,
    receivers,
    send_idx,
    send_len,
    edge_count,
    edge_w,
    edge_b,
    edge_g,
    edge_s,
    node_w,
    node_b,
    node_g,
    load_sem,
    ext,
    outgoing,
    oh_s,
    oht_s,
    oh_r,
    oht_r,
    oh_i,
    proj,
    z1,
    z2,
    a1,
    a2,
    normed_e,
    inv_e,
    low_y,
    sum_send,
    sum_recv,
    agg,
    agg_own,
    d1,
    d2,
    d3,
    back_send,
    back_recv,
    own_acc,
    own_send,
    own_recv,
    nw_stage,
    nw_recv,
    nw_zown,
    nw_z,
    nw_fown,
    nw_full,
    ea_stage,
    ea_recv,
    ea_zown,
    ea_z,
    ea_fown,
    ea_full,
    eb_stage,
    eb_recv,
    eb_zown,
    eb_z,
    eb_fown,
    eb_full,
    vec,
    vec_in,
    vec_zown,
    vec_z,
    ag_s,
    ag_r,
    halo_s,
    halo_r,
    sum_s,
    sum_r,
    agg_s,
    agg_r,
    back_s,
    back_r,
    own_s,
    own_r,
    nrs_s,
    nrs_r,
    nz_s,
    nz_r,
    nag_s,
    nag_r,
    ars_s,
    ars_r,
    az_s,
    az_r,
    aag_s,
    aag_r,
    brs_s,
    brs_r,
    bz_s,
    bz_r,
    bag_s,
    bag_r,
    vrs_s,
    vrs_r,
    vz_s,
    vz_r,
):
    loads = {}
    for name, src, dst in (
        ("node_lat", hbm_node_lat, node_lat),
        ("edge_lat", hbm_edge_lat, edge_lat),
        ("node_cot", hbm_node_cot, node_cot),
        ("edge_cot", hbm_edge_cot, edge_cot),
        ("senders", hbm_senders, senders),
        ("receivers", hbm_receivers, receivers),
        ("send_idx", hbm_send_idx, send_idx),
        ("send_len", hbm_send_len, send_len),
        ("edge_count", hbm_edge_count, edge_count),
        ("edge_w", hbm_edge_w, edge_w),
        ("edge_b", hbm_edge_b, edge_b),
        ("edge_g", hbm_edge_g, edge_g),
        ("edge_s", hbm_edge_s, edge_s),
        ("node_w", hbm_node_w, node_w),
        ("node_b", hbm_node_b, node_b),
        ("node_g", hbm_node_g, node_g),
    ):
        loads[name] = pltpu.make_async_copy(src, dst, load_sem.at[len(loads)])
        loads[name].start()

    stores = []

    def store(src, dst):
        stores.append(pltpu.make_async_copy(src, dst, store_sem.at[len(stores)]))
        stores[-1].start()

    def ready(*wanted):
        for name in wanted:
            loads[name].wait()

    dom, n_edge, n_sub = sizes
    inner = n_edge * n_sub
    rows = node_lat.shape[0]
    edges = edge_lat.shape[0]
    part_rows = rows * inner
    blocks, slot = send_idx.shape
    ext_rows = part_rows + blocks * slot
    reach = blocks // 2
    offsets = [b - reach if b < reach else b - reach + 1 for b in range(blocks)]
    my_dom = lax.axis_index("dom")
    me = lax.axis_index("edge") * n_sub + lax.axis_index("sub")
    width = LANES // inner
    pending = []

    def inner_id(position):
        return {"edge": position // n_sub, "sub": position % n_sub}

    def remote(src, dst, send, recv, where):
        return pltpu.make_async_remote_copy(
            src_ref=src,
            dst_ref=dst,
            send_sem=send,
            recv_sem=recv,
            device_id=where,
            device_id_type=pl.DeviceIdType.MESH,
        )

    def inner_start(pick_src, pick_dst, send, recv):
        copies = []
        for o in range(1, inner):
            target = (me + o) % inner
            copy = remote(
                pick_src(target, o), pick_dst(me, o), send.at[o], recv.at[o], inner_id(target)
            )
            copy.start()
            copies.append(copy)
            pending.append(copy)
        return copies

    def dom_start(src, pick_dst, send, recv):
        copies = []
        for o in range(1, dom):
            target = (my_dom + o) % dom
            copy = remote(src, pick_dst(my_dom, o), send.at[o], recv.at[o], {"dom": target})
            copy.start()
            copies.append(copy)
            pending.append(copy)
        return copies

    def arrive(copies):
        for copy in copies:
            copy.wait_recv()

    def part_slice(position):
        return pl.ds(pl.multiple_of(position * rows, rows), rows)

    def wslice(position):
        return pl.ds(pl.multiple_of(position * width, width), width)

    barrier = pltpu.get_barrier_semaphore()
    for o in range(1, inner):
        pl.semaphore_signal(
            barrier,
            inc=1,
            device_id=inner_id((me + o) % inner),
            device_id_type=pl.DeviceIdType.MESH,
        )
    for o in range(1, dom):
        pl.semaphore_signal(
            barrier,
            inc=1,
            device_id={"dom": (my_dom + o) % dom},
            device_id_type=pl.DeviceIdType.MESH,
        )
    pl.semaphore_wait(barrier, inner - 1 + dom - 1)

    ready("node_lat")
    gathered = inner_start(
        lambda target, o: node_lat, lambda mine, o: ext.at[part_slice(mine)], ag_s, ag_r
    )
    ext[part_slice(me), :] = node_lat[...]

    lane = lax.broadcasted_iota(jnp.int32, (LANES, LANES), 1)
    sublane = lax.broadcasted_iota(jnp.int32, (LANES, LANES), 0)

    ready("send_idx", "send_len", "senders", "receivers")

    def columns_of(row):
        return jnp.transpose(jnp.broadcast_to(row, (LANES, LANES)))

    def hot(mask):
        return jnp.where(mask, 1.0, 0.0).astype(BF16)

    for b in range(blocks):
        row = jnp.where(lane[:1] < send_len[:, b : b + 1], send_idx[b : b + 1, :], -1)
        column = columns_of(row)
        for t in range(0, part_rows, LANES):
            oh_i[b * slot : (b + 1) * slot, t : t + LANES] = hot(column == lane + t)

    for c in range(edges // LANES):
        span = slice(c * LANES, (c + 1) * LANES)
        row_r = receivers[c : c + 1, :]
        column_r = columns_of(row_r)
        for t in range(0, part_rows, LANES):
            oh_r[span, t : t + LANES] = hot(column_r == lane + t)
            oht_r[t : t + LANES, span] = hot(row_r == sublane + t)
        row_s = senders[c : c + 1, :]
        column_s = columns_of(row_s)
        for t in range(0, ext_rows, LANES):
            oh_s[span, t : t + LANES] = hot(column_s == lane + t)
            oht_s[t : t + LANES, span] = hot(row_s == sublane + t)

    ready(
        "edge_lat", "edge_cot", "edge_count", "edge_w", "edge_b", "edge_g", "edge_s",
        "node_cot", "node_w", "node_b", "node_g",
    )
    arrive(gathered)

    outgoing[...] = nn(oh_i[...], ext[:part_rows, :]).astype(BF16)
    halo = []
    for b in range(blocks):
        target = my_dom + offsets[b]
        source = my_dom - offsets[b]
        has_target = (target >= 0) & (target < dom)
        has_source = (source >= 0) & (source < dom)
        region = ext.at[part_rows + b * slot : part_rows + (b + 1) * slot]
        copy = remote(
            outgoing.at[b * slot : (b + 1) * slot],
            region,
            halo_s.at[b],
            halo_r.at[b],
            {"dom": lax.clamp(0, target, dom - 1)},
        )
        pl.when(has_target)(copy.start)

        @pl.when(jnp.logical_not(has_source))
        def _(region=region):
            region[...] = jnp.zeros(region.shape, BF16)

        halo.append((copy, has_target, has_source))

    proj[part_rows + blocks * slot :, :] = nn(ext[:part_rows, :], edge_w[2]).astype(BF16)
    proj[:part_rows, :] = nn(ext[:part_rows, :], edge_w[1]).astype(BF16)
    for c in range(0, edges, CHUNK):
        span = slice(c, c + CHUNK)
        z1[span, :] = (
            nn(edge_lat[span, :], edge_w[0])
            + nn(oh_r[span, :], proj[ext_rows:, :])
            + nn(oh_s[span, :part_rows], proj[:part_rows, :])
            + edge_b[0:1, :]
        )

    for copy, has_target, has_source in halo:
        pl.when(has_source)(copy.wait_recv)
    proj[part_rows:ext_rows, :] = nn(ext[part_rows:, :], edge_w[1]).astype(BF16)

    for c in range(0, edges, CHUNK):
        span = slice(c, c + CHUNK)
        first = z1[span, :] + nn(oh_s[span, part_rows:], proj[part_rows:ext_rows, :])
        z1[span, :] = first
        act1 = silu(first).astype(BF16)
        a1[span, :] = act1
        second = nn(act1, edge_w[3]) + edge_b[1:2, :]
        z2[span, :] = second
        act2 = silu(second).astype(BF16)
        a2[span, :] = act2
        normed, inv_std = normalise(nn(act2, edge_w[4]) + edge_b[2:3, :])
        normed_e[span, :] = normed
        inv_e[span, :] = inv_std
        valid = lax.broadcasted_iota(jnp.int32, (CHUNK, 1), 0) + c < edge_count[...]
        low_y[span, :] = jnp.where(valid, normed * edge_g[...] + edge_s[...], 0.0).astype(BF16)

    own_acc[...] = nn(oht_r[...], low_y[...])
    sum_send[...] = own_acc[...].astype(BF16)
    summing = inner_start(
        lambda target, o: sum_send.at[part_slice(target)],
        lambda mine, o: sum_recv.at[o],
        sum_s,
        sum_r,
    )

    z1[...] = slope_of(z1[...])
    z2[...] = slope_of(z2[...])
    node_base = nn(node_lat[...], node_w[0]) + node_b[0:1, :]
    cot_n = node_cot[...].astype(F32)

    arrive(summing)
    total = own_acc[part_slice(me), :]
    for o in range(1, inner):
        total = total + sum_recv[o].astype(F32)
    total_low = total.astype(BF16)

    pre1 = node_base + nn(total_low, node_w[1])
    n1 = silu(pre1).astype(BF16)
    pre2 = nn(n1, node_w[2]) + node_b[1:2, :]
    n2 = silu(pre2).astype(BF16)
    normed_n, inv_n = normalise(nn(n2, node_w[3]) + node_b[2:3, :])
    g3 = norm_backward(cot_n * node_g[...], normed_n, inv_n)
    g3_low = g3.astype(BF16)
    g2 = nt(g3_low, node_w[3]) * slope_of(pre2)
    g2_low = g2.astype(BF16)
    g1 = nt(g2_low, node_w[2]) * slope_of(pre1)
    g1_low = g1.astype(BF16)
    agg_own[...] = nt(g1_low, node_w[1]).astype(BF16)
    aggregating = inner_start(
        lambda target, o: agg_own, lambda mine, o: agg.at[part_slice(mine)], agg_s, agg_r
    )
    agg[part_slice(me), :] = agg_own[...]

    out_nodes[...] = cot_n + nt(g1_low, node_w[0])
    nw_stage[0] = tn(node_lat[...], g1_low).astype(BF16)
    nw_stage[1] = tn(total_low, g1_low).astype(BF16)
    nw_stage[2] = tn(n1, g2_low).astype(BF16)
    nw_stage[3] = tn(n2, g3_low).astype(BF16)
    vec[8:9, :] = column_sum(g1)
    vec[9:10, :] = column_sum(g2)
    vec[10:11, :] = column_sum(g3)
    vec[11:12, :] = column_sum(cot_n * normed_n)
    vec[12:16, :] = jnp.zeros((4, LANES), F32)
    vec[5:8, :] = jnp.zeros((3, LANES), F32)

    def reduce_start(stage, recv, send, got):
        return inner_start(
            lambda target, o: stage.at[:, wslice(target), :],
            lambda mine, o: recv.at[o],
            send,
            got,
        )

    def reduce_finish(stage, recv, zown, z, send, got):
        partial = stage[:, wslice(me), :].astype(F32)
        for o in range(1, inner):
            partial = partial + recv[o].astype(F32)
        partial = partial.astype(BF16)
        zown[...] = partial
        z[my_dom] = partial
        return dom_start(zown, lambda mine, o: z.at[mine], send, got)

    def gather_start(z, fown, full, send, got):
        partial = z[0].astype(F32)
        for d in range(1, dom):
            partial = partial + z[d].astype(F32)
        partial = partial.astype(BF16)
        fown[...] = partial
        full[:, wslice(me), :] = partial
        return inner_start(
            lambda target, o: fown, lambda mine, o: full.at[:, wslice(mine), :], send, got
        )

    node_rs = reduce_start(nw_stage, nw_recv, nrs_s, nrs_r)

    arrive(aggregating)
    sums = [jnp.zeros((1, LANES), F32) for _ in range(5)]
    for c in range(0, edges, CHUNK):
        span = slice(c, c + CHUNK)
        valid = lax.broadcasted_iota(jnp.int32, (CHUNK, 1), 0) + c < edge_count[...]
        cot = edge_cot[span, :].astype(F32)
        dy = jnp.where(valid, cot + nn(oh_r[span, :], agg[...]), 0.0)
        if c == edges // CHUNK // 2 * CHUNK:
            arrive(node_rs)
            node_z = reduce_finish(nw_stage, nw_recv, nw_zown, nw_z, nz_s, nz_r)
        normed = normed_e[span, :]
        h3 = norm_backward(dy * edge_g[...], normed, inv_e[span, :])
        h3_low = h3.astype(BF16)
        d3[span, :] = h3_low
        h2 = nt(h3_low, edge_w[4]) * z2[span, :]
        h2_low = h2.astype(BF16)
        d2[span, :] = h2_low
        h1 = nt(h2_low, edge_w[3]) * z1[span, :]
        h1_low = h1.astype(BF16)
        d1[span, :] = h1_low
        out_edges[span, :] = (cot + nt(h1_low, edge_w[0])).astype(BF16)
        for position, term in enumerate((h1, h2, h3, dy * normed, dy)):
            sums[position] = sums[position] + column_sum(term)

    store(out_edges, hbm_out_edges)
    for position in range(5):
        vec[position : position + 1, :] = sums[position]
    vec_in[me] = vec[...]
    vec_rs = inner_start(lambda target, o: vec, lambda mine, o: vec_in.at[mine], vrs_s, vrs_r)

    back_send[...] = nn(oht_s[part_rows:, :], d1[...]).astype(BF16)
    returning = []
    for b in range(blocks):
        target = my_dom - offsets[b]
        source = my_dom + offsets[b]
        has_target = (target >= 0) & (target < dom)
        has_source = (source >= 0) & (source < dom)
        region = back_recv.at[b * slot : (b + 1) * slot]
        copy = remote(
            back_send.at[b * slot : (b + 1) * slot],
            region,
            back_s.at[b],
            back_r.at[b],
            {"dom": lax.clamp(0, target, dom - 1)},
        )
        pl.when(has_target)(copy.start)

        @pl.when(jnp.logical_not(has_source))
        def _(region=region):
            region[...] = jnp.zeros(region.shape, BF16)

        returning.append((copy, has_target, has_source))

    ea_stage[0] = tn(edge_lat[...], d1[...]).astype(BF16)
    ea_stage[1] = tn(a1[...], d2[...]).astype(BF16)
    ea_stage[2] = tn(a2[...], d3[...]).astype(BF16)
    ea_rs = reduce_start(ea_stage, ea_recv, ars_s, ars_r)
    own_low = nn(oht_s[:part_rows, :], d1[...]).astype(BF16)
    recv_low = nn(oht_r[...], d1[...]).astype(BF16)
    eb_stage[0] = (tn(ext[:part_rows, :], own_low) + tn(ext[part_rows:, :], back_send[...])).astype(
        BF16
    )
    eb_stage[1] = tn(ext[:part_rows, :], recv_low).astype(BF16)
    eb_rs = reduce_start(eb_stage, eb_recv, brs_s, brs_r)
    own_acc[...] = nt(own_low, edge_w[1]) + nt(recv_low, edge_w[2])

    arrive(ea_rs)
    ea_zs = reduce_finish(ea_stage, ea_recv, ea_zown, ea_z, az_s, az_r)

    for copy, has_target, has_source in returning:
        pl.when(has_source)(copy.wait_recv)
    scattered = tn(oh_i[...], back_recv[...]).astype(BF16)
    own_acc[...] = own_acc[...] + nt(scattered, edge_w[1])
    own_send[...] = own_acc[...].astype(BF16)
    owning = inner_start(
        lambda target, o: own_send.at[part_slice(target)],
        lambda mine, o: own_recv.at[o],
        own_s,
        own_r,
    )

    arrive(eb_rs)
    eb_zs = reduce_finish(eb_stage, eb_recv, eb_zown, eb_z, bz_s, bz_r)
    arrive(vec_rs)
    vec_sum = vec_in[0]
    for position in range(1, inner):
        vec_sum = vec_sum + vec_in[position]
    vec_zown[...] = vec_sum
    vec_z[my_dom] = vec_sum
    vec_all = dom_start(vec_zown, lambda mine, o: vec_z.at[mine], vz_s, vz_r)

    arrive(node_z)
    node_ag = gather_start(nw_z, nw_fown, nw_full, nag_s, nag_r)

    arrive(ea_zs)
    ea_ag = gather_start(ea_z, ea_fown, ea_full, aag_s, aag_r)
    arrive(eb_zs)
    eb_ag = gather_start(eb_z, eb_fown, eb_full, bag_s, bag_r)

    arrive(owning)
    mine = own_acc[part_slice(me), :]
    for o in range(1, inner):
        mine = mine + own_recv[o].astype(F32)
    out_nodes[...] = out_nodes[...] + mine
    store(out_nodes, hbm_out_nodes)

    edge_scale = 1.0 / math.sqrt(edges * dom * inner)
    node_scale = 1.0 / math.sqrt(rows * dom * inner)
    arrive(vec_all)
    vec_sum = vec_z[0]
    for d in range(1, dom):
        vec_sum = vec_sum + vec_z[d]
    out_vec[0:8, :] = vec_sum[0:8, :] * edge_scale
    out_vec[8:16, :] = vec_sum[8:16, :] * node_scale
    store(out_vec, hbm_out_vec)
    arrive(node_ag)
    out_nw[...] = nw_full[...].astype(F32) * node_scale
    store(out_nw, hbm_out_nw)
    arrive(ea_ag)
    out_ew[0] = ea_full[0].astype(F32) * edge_scale
    out_ew[3:5] = ea_full[1:3].astype(F32) * edge_scale
    arrive(eb_ag)
    out_ew[1:3] = eb_full[...].astype(F32) * edge_scale
    store(out_ew, hbm_out_ew)

    for copy in stores:
        copy.wait()
    for copy in pending:
        copy.wait_send()
    for copy, has_target, has_source in halo + returning:
        pl.when(has_target)(copy.wait_send)


def store_kernel(
    nodes,
    edges,
    ew,
    nw,
    vec,
    out_nodes,
    out_edges,
    out_ew,
    out_ev,
    out_nw,
    out_nv,
    v_nodes,
    v_edges,
    v_ew,
    v_nw,
    v_ev,
    v_nv,
    load_sem,
    store_sem,
):
    routes = (
        (vec.at[0:5], v_ev, out_ev),
        (vec.at[8:12], v_nv, out_nv),
        (nodes, v_nodes, out_nodes),
        (edges, v_edges, out_edges),
        (nw, v_nw, out_nw),
        (ew, v_ew, out_ew),
    )
    loads = [
        pltpu.make_async_copy(src, mid, load_sem.at[position])
        for position, (src, mid, _) in enumerate(routes)
    ]
    stores = [
        pltpu.make_async_copy(mid, dst, store_sem.at[position])
        for position, (_, mid, dst) in enumerate(routes)
    ]
    for copy in loads:
        copy.start()
    for load, copy in zip(loads, stores):
        load.wait()
        copy.start()
    for copy in stores:
        copy.wait()


def local(sizes, *arrays):
    (
        node_lat,
        edge_lat,
        node_cot,
        edge_cot,
        senders,
        receivers,
        send_idx,
        send_len,
        edge_count,
        edge_w,
        edge_b,
        edge_g,
        edge_s,
        node_w,
        node_b,
        node_g,
    ) = arrays
    dom, n_edge, n_sub = sizes
    inner = n_edge * n_sub
    rows, features = node_lat.shape
    edges = edge_lat.shape[0]
    blocks, slot = send_idx.shape[1:]
    part_rows = rows * inner
    ext_rows = part_rows + blocks * slot
    width = features // inner
    operands = (
        node_lat,
        edge_lat,
        node_cot,
        edge_cot,
        senders.reshape(edges // LANES, LANES),
        receivers.reshape(edges // LANES, LANES),
        send_idx[0],
        send_len,
        edge_count,
        edge_w,
        edge_b,
        edge_g.reshape(1, features),
        edge_s.reshape(1, features),
        node_w,
        node_b,
        node_g.reshape(1, features),
    )
    hbm = pl.BlockSpec(memory_space=pltpu.HBM)

    def low(*shape):
        return pltpu.VMEM(shape + (features,), BF16)

    def full(*shape):
        return pltpu.VMEM(shape + (features,), F32)

    def weights(count):
        return [
            low(count, features),
            low(inner, count, width),
            low(count, width),
            low(dom, count, width),
            low(count, width),
            low(count, features),
        ]

    def sems(count):
        return [pltpu.SemaphoreType.DMA((count,)), pltpu.SemaphoreType.DMA((count,))]

    scratch = [
        full(rows),
        low(edges),
        full(5, features),
        full(4, features),
        full(16),
        pltpu.SemaphoreType.DMA((5,)),
        *[pltpu.VMEM(array.shape, array.dtype) for array in operands],
        pltpu.SemaphoreType.DMA((len(operands),)),
        low(ext_rows),
        low(blocks * slot),
        pltpu.VMEM((edges, ext_rows), BF16),
        pltpu.VMEM((ext_rows, edges), BF16),
        pltpu.VMEM((edges, part_rows), BF16),
        pltpu.VMEM((part_rows, edges), BF16),
        pltpu.VMEM((blocks * slot, part_rows), BF16),
        low(ext_rows + part_rows),
        full(edges),
        full(edges),
        low(edges),
        low(edges),
        full(edges),
        pltpu.VMEM((edges, 1), F32),
        low(edges),
        low(part_rows),
        low(inner, rows),
        low(part_rows),
        low(rows),
        low(edges),
        low(edges),
        low(edges),
        low(blocks * slot),
        low(blocks * slot),
        full(part_rows),
        low(part_rows),
        low(inner, rows),
        *weights(4),
        *weights(3),
        *weights(2),
        full(16),
        full(inner, 16),
        full(16),
        full(dom, 16),
        *sems(inner),
        *sems(blocks),
        *sems(inner),
        *sems(inner),
        *sems(blocks),
        *sems(inner),
        *sems(inner),
        *sems(dom),
        *sems(inner),
        *sems(inner),
        *sems(dom),
        *sems(inner),
        *sems(inner),
        *sems(dom),
        *sems(inner),
        *sems(inner),
        *sems(dom),
    ]
    results = pl.pallas_call(
        functools.partial(kernel, sizes),
        out_shape=(
            jax.ShapeDtypeStruct((rows, features), F32),
            jax.ShapeDtypeStruct((edges, features), BF16),
            jax.ShapeDtypeStruct((5, features, features), F32),
            jax.ShapeDtypeStruct((4, features, features), F32),
            jax.ShapeDtypeStruct((16, features), F32),
        ),
        in_specs=[hbm] * len(operands),
        out_specs=(hbm,) * 5,
        scratch_shapes=scratch,
        compiler_params=pltpu.CompilerParams(
            collective_id=0, has_side_effects=True, vmem_limit_bytes=VMEM_BYTES
        ),
    )(*operands)
    return pl.pallas_call(
        store_kernel,
        out_shape=(
            jax.ShapeDtypeStruct((rows, features), F32),
            jax.ShapeDtypeStruct((edges, features), BF16),
            jax.ShapeDtypeStruct((5, features, features), F32),
            jax.ShapeDtypeStruct((5, features), F32),
            jax.ShapeDtypeStruct((4, features, features), F32),
            jax.ShapeDtypeStruct((4, features), F32),
        ),
        in_specs=[hbm] * 5,
        out_specs=(hbm,) * 6,
        scratch_shapes=[
            full(rows),
            low(edges),
            full(5, features),
            full(4, features),
            full(5),
            full(4),
            pltpu.SemaphoreType.DMA((6,)),
            pltpu.SemaphoreType.DMA((6,)),
        ],
        compiler_params=pltpu.CompilerParams(vmem_limit_bytes=VMEM_BYTES),
    )(*results)


def solution(mesh):
    sizes = (mesh.shape["dom"], mesh.shape["edge"], mesh.shape["sub"])
    part = P(("groups", "dom", "edge", "sub"), None)
    index = P(("groups", "dom", "edge", "sub"))
    return jax.shard_map(
        functools.partial(local, sizes),
        mesh=mesh,
        in_specs=(
            part,
            part,
            part,
            part,
            index,
            index,
            P(("groups", "dom"), None, None),
            P(("groups", "dom"), None),
            P(("groups", "dom"), ("edge", "sub")),
        )
        + (P(),) * 7,
        out_specs=(
            part,
            part,
            P("groups", None, None),
            P("groups", None),
            P("groups", None, None),
            P("groups", None),
        ),
        check_vma=False,
    )
```
